768 devices in a mesh: wide: 32 (over x, y_hi, core), cell: 24 (over z, y_lo).
Axes of the slice: x: 4, y: 8 (y_hi: 4, y_lo: 2; y = y_hi * 2 + y_lo), z: 12, core: 2. Of those that a mesh axis runs over, the one named last changes fastest.
Arguments:
- green_pair: float32 [2, 2, 128, 24, 128, 128], P(None, None, 'wide', 'cell'), may hold values from -5 to 5
- coulomb: float32 [24, 2, 128, 128], P('cell'), may hold values from -0.5 to 0.5
- green_retarded: float32 [2, 128, 24, 2, 128, 128], P(None, 'wide', 'cell'), may hold values from -0.375 to 0.375
- offsets: int32 [24, 2], P('cell'), may hold values from -1 to 1, as said below
Outputs:
- dressed: float32 [2, 128, 24, 128, 128], P(None, 'wide', 'cell')
The draws below stay inside these ranges and needn't reach their ends.
Inputs may be any that keep to these rules, and one draw needn't show every extreme that they name: Block row r stores its blocks at block columns r + offsets[r, 0] and r + offsets[r, 1], two different entries of -1, 0, 1 in increasing order. Every block row r with r even has offsets -1 and 1.
All inputs are finite; a program needn't handle non-finite values.
Results may differ from the reference program's by a relative error of at most 0.00014.
Values sent between devices are 32-bit elements; how exact they have to be, the bound alone decides.
A program may use at most 32 MiB of HBM per device.

```python
import math
import jax
import jax.numpy as jnp
from jax import lax

B = 128
BR_DEV = 1
NE = 128
NB = 24


def draw_offsets(key, part):
    absent = jax.random.randint(key, (NB,), 0, 3)
    rows_all = jnp.arange(NB, dtype=jnp.int32)
    owner_even = rows_all // BR_DEV % 2 == 0
    local_place = rows_all % BR_DEV
    at_edge = jnp.logical_or(local_place == 0, local_place == BR_DEV - 1)
    forced = jnp.logical_and(owner_even, at_edge)
    absent = jnp.where(forced, 1, absent)
    below_slot = jnp.where(absent == 0, 0, -1)
    above_slot = jnp.where(absent == 2, 0, 1)
    return jnp.stack([below_slot, above_slot], axis=1).astype(jnp.int32)


def level_of(key, dims, cuts, low, high):
    factor_of, own = 1.0, jax.random.fold_in(key, 6)
    for dim, parts in cuts:
        heights = jnp.exp(jax.random.uniform(jax.random.fold_in(own, dim), (parts,), jnp.float32, low / len(cuts), high / len(cuts)))
        factor_of = factor_of * jnp.repeat(heights, dims[dim] // parts).reshape([-1 if axis == dim else 1 for axis in range(len(dims))])
    return factor_of


def bell_draw(rng, extent, deviation, most, shards=(), kind=jnp.bfloat16):
    result = jax.random.normal(rng, extent, jnp.float32) * deviation
    if len(shards) > 0:
        result = level_of(rng, extent, shards, -0.22, 0.18) * result
    return jnp.clip(result, min=-most, max=most).astype(kind)


def setup_inputs(seed: int = 0) -> dict:
    splits = jax.random.split(jax.random.key(seed), 5)
    return {
        "green_pair": bell_draw(splits[0], (2, 2, NE, NB, B, B), 0.7, 5.0, ((2, 32), (3, 24)), jnp.float32),
        "coulomb": bell_draw(splits[1], (NB, 2, B, B), B ** -0.5, 0.5, ((0, 24),), jnp.float32),
        "green_retarded": bell_draw(splits[2], (2, NE, NB, 2, B, B), (2 * B) ** -0.5, 0.375, ((1, 32), (2, 24)), jnp.float32),
        "offsets": draw_offsets(jax.random.fold_in(splits[4], 71), 0),
    }


def reference(green_pair, coulomb, green_retarded, offsets):
    period = 2 * NE
    lesser = jnp.moveaxis(green_pair[0, 0] + 1j * green_pair[0, 1], 1, 0)
    greater = jnp.moveaxis(green_pair[1, 0] + 1j * green_pair[1, 1], 1, 0)

    def polarize(couple):
        low_part, high_part = couple
        spectrum = jnp.fft.fft(low_part, period, axis=0) * jnp.fft.ifft(high_part, period, axis=0) * period
        return jnp.roll(jnp.fft.ifft(spectrum, axis=0), NE, axis=0) / math.sqrt(NE)
    polar_all = lax.map(polarize, (lesser, greater))
    polar_padded = jnp.pad(polar_all, ((1, 1), (0, 0), (0, 0), (0, 0)))

    def self_energy(block_row):
        screened = jnp.zeros((period, B, B), polar_all.dtype)
        for position in range(2):
            column = block_row + 1 + offsets[block_row, position]
            neighbour = lax.dynamic_index_in_dim(polar_padded, column, 0, keepdims=False)
            coupling = coulomb[block_row, position]
            screened = screened + jnp.einsum('ab,qbc,dc->qad', coupling, neighbour, coupling, precision=lax.Precision.HIGHEST)
        circular = jnp.roll(screened, -NE, axis=0)
        spectrum = jnp.fft.fft(lesser[block_row], period, axis=0) * jnp.fft.fft(circular, axis=0)
        return jnp.fft.ifft(spectrum, axis=0)[:NE] / math.sqrt(NE)
    rows_all = jnp.arange(NB, dtype=jnp.int32)
    sigma_all = lax.map(self_energy, rows_all)
    sigma_padded = jnp.pad(sigma_all, ((1, 1), (0, 0), (0, 0), (0, 0)))
    retarded = jnp.moveaxis(green_retarded[0] + 1j * green_retarded[1], 1, 0)

    def dressed_row(block_row):
        running = jnp.zeros((NE, B, B), sigma_all.dtype)
        for position in range(2):
            column = block_row + 1 + offsets[block_row, position]
            neighbour = lax.dynamic_index_in_dim(sigma_padded, column, 0, keepdims=False)
            green_block = retarded[block_row][:, position]
            running = running + jnp.einsum('nab,nbc,ndc->nad', green_block, neighbour, green_block, precision=lax.Precision.HIGHEST)
        return running
    dressed_all = jnp.moveaxis(lax.map(dressed_row, rows_all), 0, 1)
    return jnp.stack([dressed_all.real, dressed_all.imag]).astype(jnp.float32)
```

```python
import functools
import math

import jax
import jax.numpy as jnp
import numpy as np
from jax import lax
from jax.experimental import pallas as pl
from jax.experimental.pallas import tpu as pltpu
from jax.sharding import PartitionSpec as P

F32 = jnp.float32
BF16 = jnp.bfloat16
MESH = pl.DeviceIdType.MESH
WIDE_PARTS = (4, 4, 2)
LOCAL = 4


def split(value):
    high = value.astype(BF16)
    return high, (value - high.astype(F32)).astype(BF16)


def dot3(first, second, transposed=False):
    dims = (((1,), (1 if transposed else 0,)), ((), ()))
    multiply = functools.partial(lax.dot_general, dimension_numbers=dims, preferred_element_type=F32)
    return multiply(first[0], second[0]) + (multiply(first[0], second[1]) + multiply(first[1], second[0]))


def tables(energies, tile):
    period = 2 * energies
    angle = np.outer(np.arange(period), np.arange(energies)) % period * (2.0 * math.pi / period)
    cos, sin = np.cos(angle), np.sin(angle)
    real = np.concatenate([cos, sin], axis=1).reshape(period // tile, tile, period)
    imag = np.concatenate([-sin, cos], axis=1).reshape(period // tile, tile, period)
    forward = np.concatenate([real, imag], axis=1)
    scale = 1.0 / (period * energies)
    inverse = scale * np.stack([np.concatenate([cos.T, -sin.T], axis=1), np.concatenate([sin.T, cos.T], axis=1)])
    result = []
    for table in (forward, inverse):
        table = table.astype(np.float32)
        high = table.astype(BF16)
        result += [high, (table - high.astype(np.float32)).astype(BF16)]
    return result


def kernel(
    green, coulomb, offsets, retarded, fwd_hi, fwd_lo, inv_hi, inv_lo, out,
    pack, pairs, lhat, psend, precv, below, above, vboth, vhi, vlo, sel, yy, zsend, srecv, qsend, sig, sigh, sigc,
    local_sem, small_send, small_recv, send_sem, a_sem, p_sem, up_sem, down_sem, s_sem, q_sem, h_sem, c_sem, fwd_sem,
):
    wide, cell = lax.axis_index("wide"), lax.axis_index("cell")
    cells = lax.axis_size("cell")
    nx, nh, nc = WIDE_PARTS
    ny = 2 * nh
    group = nx * nc
    plane = ny * group
    energies = green.shape[2] * nx * nh * nc
    times = 2 * energies
    order = green.shape[-1]
    core, yh, x = wide % nc, wide // nc % nh, wide // (nc * nh)
    yl, z = cell % 2, cell // 2
    y = 2 * yh + yl
    place = (y * nx + x) * nc + core
    up = (wide, (cell + 2) % cells)
    down = (wide, (cell + cells - 2) % cells)
    partner = (wide, cell + 1 - 2 * yl)

    def rows8(index):
        return pl.ds(pl.multiple_of(8 * index, 8), 8)

    def rise(g):
        return jnp.where(g % 2 == 1, (g + 1) // 2, (ny - g // 2) % ny)

    def peer(k):
        g, h = k // group, k % group
        y2, x2, c2 = (y + rise(g)) % ny, (x + h // nc) % nx, (core + h % nc) % nc
        return g, (x2 * nh + y2 // 2) * nc + c2, y2 % 2, (y2 * nx + x2) * nc + c2

    def remote(src, dst, send, recv, device):
        return pltpu.make_async_remote_copy(
            src_ref=src, dst_ref=dst, send_sem=send, recv_sem=recv, device_id=device, device_id_type=MESH
        )

    def await_bytes(like, sem):
        pltpu.make_async_copy(like, like, sem).wait()

    def chunk(g):
        y0 = (y + ny - rise(g)) % ny
        return pl.ds(pl.multiple_of(y0 * (8 * group), 8 * group), 8 * group)

    barrier = pltpu.get_barrier_semaphore()

    def greet(k, carry):
        g, wide2, yl2, place2 = peer(k)
        pl.semaphore_signal(barrier, inc=1, device_id=(wide2, 2 * z + yl2), device_id_type=MESH)
        return carry

    lax.fori_loop(1, plane, greet, 0)
    for device in (up, down):
        pl.semaphore_signal(barrier, inc=1, device_id=device, device_id_type=MESH)

    for pair in range(2):
        for part in range(2):
            for e in range(LOCAL):
                for i in range(2):
                    pack[pair, part, pl.ds(2 * e + i, plane, stride=8), :] = green[
                        pair, part, e, i * plane : (i + 1) * plane, :
                    ]
    for slot in range(2):
        sel[yl, slot] = jnp.where(jnp.full((8, order), offsets[0, slot], jnp.int32) != 0, 1.0, 0.0)
    vboth[yl] = coulomb[...]
    pl.semaphore_wait(barrier, plane + 1)

    def send_pairs(k, carry):
        g, wide2, yl2, place2 = peer(k)
        remote(
            pack.at[:, :, rows8(place2), :], pairs.at[:, :, yl, rows8(wide), :],
            send_sem.at[0], a_sem, (wide2, 2 * z + yl2),
        ).start()
        return carry

    lax.fori_loop(1, plane, send_pairs, 0)
    own = pltpu.make_async_copy(pack.at[:, :, rows8(place), :], pairs.at[:, :, yl, rows8(wide), :], local_sem.at[0])
    own.start()
    coulomb_copy = remote(vboth.at[yl], vboth.at[yl], small_send.at[0], small_recv.at[0], partner)
    coulomb_copy.start()
    masks_copy = remote(sel.at[yl], sel.at[yl], small_send.at[1], small_recv.at[1], partner)
    masks_copy.start()

    @pl.when(yl == 0)
    def _():
        sigc[...] = jnp.zeros_like(sigc)

    own.wait()
    await_bytes(pack.at[:, :, pl.ds(0, 8 * plane - 8), :], a_sem)

    tiles, tile = fwd_hi.shape[0], fwd_hi.shape[1] // 2

    def transform(r, carry):
        for i in range(2):
            lr, li, ur, ui = (pairs[a, b, r, pl.ds(i, energies, stride=2), :] for a in range(2) for b in range(2))
            rhs = split(jnp.concatenate([jnp.concatenate([lr, ur], 1), jnp.concatenate([li, -ui], 1)], 0))
            for m in range(tiles):
                both = dot3((fwd_hi[m], fwd_lo[m]), rhs)
                ar, ai = both[:tile, :order], both[tile:, :order]
                br, bi = both[:tile, order:], both[tile:, order:]
                rows = pl.ds(2 * m * tile + i, tile, stride=2)
                lhat[0, r, rows, :] = ar
                lhat[1, r, rows, :] = ai
                psend[0, r, rows, :] = ar * br + ai * bi
                psend[1, r, rows, :] = ai * br - ar * bi
        return carry

    lax.fori_loop(0, 2, transform, 0)

    def send_polar(k, carry):
        g, wide2, yl2, place2 = peer(k)
        remote(
            psend.at[:, :, rows8(place2), :], precv.at[:, :, rows8(place), :],
            send_sem.at[1], p_sem.at[g], (wide2, 2 * z + yl2),
        ).start()
        return carry

    pltpu.make_async_copy(psend.at[:, :, rows8(place), :], precv.at[:, :, rows8(place), :], p_sem.at[0]).start()
    lax.fori_loop(1, plane, send_polar, 0)

    coulomb_copy.wait()
    masks_copy.wait()
    for r in range(2):
        for slot in range(2):
            high, low = split(vboth[r, slot])
            vhi[r, :, slot * order : (slot + 1) * order] = high
            vlo[r, :, slot * order : (slot + 1) * order] = low

    def forward(g, carry):
        rows = chunk(g)
        await_bytes(precv.at[:, :, rows, :], p_sem.at[g])
        remote(precv.at[:, 1, rows, :], below.at[:, rows, :], fwd_sem.at[0], up_sem.at[g], up).start()
        remote(precv.at[:, 0, rows, :], above.at[:, rows, :], fwd_sem.at[1], down_sem.at[g], down).start()
        return carry

    lax.fori_loop(0, ny, forward, 0)
    has_below = jnp.where(z > 0, 1.0, 0.0).astype(F32)
    has_above = jnp.where(z < cells // 2 - 1, 1.0, 0.0).astype(F32)

    def from_right(g, carry):
        rows = chunk(g)
        await_bytes(below.at[:, rows, :], up_sem.at[g])
        await_bytes(above.at[:, rows, :], down_sem.at[g])

        def stacked(ref, *lead):
            return jnp.concatenate([ref[(part, *lead, rows, slice(None))] for part in range(2)], 0)

        lower, even, odd, upper = (
            stacked(below) * has_below, stacked(precv, 0), stacked(precv, 1), stacked(above) * has_above
        )
        first = jnp.where(sel[1, 0, 0:1, :] > 0.5, even, odd)
        second = jnp.where(sel[1, 1, 0:1, :] > 0.5, upper, odd)
        for r, slot, value in ((0, 0, lower), (0, 1, odd), (1, 0, first), (1, 1, second)):
            block = slice(slot * order, (slot + 1) * order)
            done = dot3(split(value), (vhi[r, :, block], vlo[r, :, block]), True)
            half = done.shape[0] // 2
            yy[r, slot, 0, rows, :] = done[:half]
            yy[r, slot, 1, rows, :] = done[half:]
        return carry

    lax.fori_loop(0, ny, from_right, 0)

    def from_left(r, carry):
        for t in range(LOCAL):
            columns = []
            for part in range(2):
                columns.append(jnp.concatenate(
                    [yy[r, slot, part, pl.ds(2 * t + i, plane, stride=8), :] for slot in range(2) for i in range(2)], 0
                ))
            done = dot3((vhi[r], vlo[r]), split(jnp.concatenate(columns, 1)))
            for part in range(2):
                for i in range(2):
                    zsend[part, r, pl.ds(2 * t + i, plane, stride=8), :] = done[
                        i * plane : (i + 1) * plane, part * order : (part + 1) * order
                    ]
        return carry

    lax.fori_loop(0, 2, from_left, 0)

    def send_screened(k, carry):
        g, wide2, yl2, place2 = peer(k)
        remote(
            zsend.at[:, :, rows8(place2), :], srecv.at[:, :, rows8(place), :],
            send_sem.at[2], s_sem, (wide2, 2 * z + yl2),
        ).start()
        return carry

    lax.fori_loop(1, plane, send_screened, 0)
    own = pltpu.make_async_copy(zsend.at[:, :, rows8(place), :], srecv.at[:, :, rows8(place), :], local_sem.at[1])
    own.start()
    own.wait()
    await_bytes(zsend.at[:, :, pl.ds(0, 8 * plane - 8), :], s_sem)

    def back(r, carry):
        columns = []
        for i in range(2):
            rows = pl.ds(i, times, stride=2)
            lr, li, sr, si = lhat[0, r, rows, :], lhat[1, r, rows, :], srecv[0, r, rows, :], srecv[1, r, rows, :]
            columns.append(jnp.concatenate([lr * sr - li * si, lr * si + li * sr], 0))
        rhs = split(jnp.concatenate(columns, 1))
        for part in range(2):
            done = dot3((inv_hi[part], inv_lo[part]), rhs)
            for i in range(2):
                qsend[part, r, pl.ds(i, energies, stride=2), :] = done[:, i * order : (i + 1) * order]
        return carry

    lax.fori_loop(0, 2, back, 0)

    def send_sigma(k, carry):
        g, wide2, yl2, place2 = peer(k)
        remote(
            qsend.at[:, 1 - yl2, rows8(wide2), :], sig.at[:, rows8(place), :],
            send_sem.at[3], q_sem.at[g], (wide2, 2 * z + yl2),
        ).start()
        return carry

    pltpu.make_async_copy(qsend.at[:, 1 - yl, rows8(wide), :], sig.at[:, rows8(place), :], q_sem.at[0]).start()
    lax.fori_loop(1, plane, send_sigma, 0)

    along = (wide, (cell + cells + 2 - 4 * yl) % cells)

    def spread(g, carry):
        rows = chunk(g)
        await_bytes(sig.at[:, rows, :], q_sem.at[g])
        remote(sig.at[:, rows, :], sigh.at[:, rows, :], fwd_sem.at[2], h_sem.at[g], along).start()

        @pl.when(yl == 0)
        def _():
            remote(sig.at[:, rows, :], sigc.at[:, rows, :], fwd_sem.at[3], c_sem.at[g], partner).start()

        return carry

    lax.fori_loop(0, ny, spread, 0)

    @pl.when(yl == 1)
    def _():
        def arrive(g, carry):
            await_bytes(sigc.at[:, chunk(g), :], c_sem.at[g])
            return carry

        lax.fori_loop(0, ny, arrive, 0)

    even = yl == 0

    def term(e, slot, sr, si):
        gr, gi = retarded[0, e, slot], retarded[1, e, slot]
        left = dot3(
            split(jnp.concatenate([gr, gi], 1)),
            split(jnp.concatenate([jnp.concatenate([sr, si], 1), jnp.concatenate([-si, sr], 1)], 0)),
        )
        return dot3(
            split(left),
            split(jnp.concatenate([jnp.concatenate([gr, -gi], 1), jnp.concatenate([gi, gr], 1)], 0)),
            True,
        )

    def block(ref, e, part):
        return jnp.concatenate([ref[part, pl.ds(2 * e + i, plane, stride=8), :] for i in range(2)], 0)

    take_near = jnp.logical_or(jnp.full((8, order), yl, jnp.int32) == 0, sel[yl, 0] > 0.5)[0:1]
    take_far = jnp.logical_or(jnp.full((8, order), yl, jnp.int32) == 0, sel[yl, 1] > 0.5)[0:1]
    for e in range(LOCAL):
        sr, si = (jnp.where(take_near, block(sig, e, part), block(sigc, e, part)) for part in range(2))
        done = term(e, 1 - yl, sr, si)
        out[0, e] = done[:, :order]
        out[1, e] = done[:, order:]

    def arrive_far(g, carry):
        await_bytes(sigh.at[:, chunk(g), :], h_sem.at[g])
        return carry

    lax.fori_loop(0, ny, arrive_far, 0)
    has_far = jnp.where(even, has_below, has_above)
    for e in range(LOCAL):
        sr, si = (
            jnp.where(take_far, block(sigh, e, part) * has_far, block(sigc, e, part)) for part in range(2)
        )
        done = term(e, yl, sr, si)
        out[0, e] += done[:, :order]
        out[1, e] += done[:, order:]

    await_bytes(pack.at[:, :, pl.ds(0, 8 * plane - 8), :], send_sem.at[0])
    await_bytes(psend.at[:, :, pl.ds(0, 8 * plane - 8), :], send_sem.at[1])
    await_bytes(zsend.at[:, :, pl.ds(0, 8 * plane - 8), :], send_sem.at[2])
    await_bytes(sig.at[:, pl.ds(0, 8 * plane - 8), :], send_sem.at[3])
    await_bytes(below, fwd_sem.at[0])
    await_bytes(above, fwd_sem.at[1])
    await_bytes(sig, fwd_sem.at[2])

    @pl.when(yl == 0)
    def _():
        await_bytes(sig, fwd_sem.at[3])


def body(green_pair, coulomb, green_retarded, offsets):
    nx, nh, nc = WIDE_PARTS
    ny, plane = 2 * nh, 2 * nx * nh * nc
    order, local = green_pair.shape[-1], green_pair.shape[2]
    energies = local * nx * nh * nc
    tile = min(64, 2 * energies)
    full = 8 * plane
    consts = [jnp.asarray(value) for value in tables(energies, tile)]
    vmem = pl.BlockSpec(memory_space=pltpu.VMEM)
    smem = pl.BlockSpec(memory_space=pltpu.SMEM)
    dma = pltpu.SemaphoreType.DMA
    dressed = pl.pallas_call(
        kernel,
        out_shape=jax.ShapeDtypeStruct((2, local, order, order), F32),
        in_specs=[vmem, vmem, smem, vmem, vmem, vmem, vmem, vmem],
        out_specs=vmem,
        scratch_shapes=[
            pltpu.VMEM((2, 2, full, order), F32),
            pltpu.VMEM((2, 2, 2, full // 2, order), F32),
            pltpu.VMEM((2, 2, full, order), F32),
            pltpu.VMEM((2, 2, full, order), F32),
            pltpu.VMEM((2, 2, full, order), F32),
            pltpu.VMEM((2, full, order), F32),
            pltpu.VMEM((2, full, order), F32),
            pltpu.VMEM((2, 2, order, order), F32),
            pltpu.VMEM((2, order, 2 * order), BF16),
            pltpu.VMEM((2, order, 2 * order), BF16),
            pltpu.VMEM((2, 2, 8, order), F32),
            pltpu.VMEM((2, 2, 2, full, order), F32),
            pltpu.VMEM((2, 2, full, order), F32),
            pltpu.VMEM((2, 2, full, order), F32),
            pltpu.VMEM((2, 2, full // 2, order), F32),
            pltpu.VMEM((2, full, order), F32),
            pltpu.VMEM((2, full, order), F32),
            pltpu.VMEM((2, full, order), F32),
            dma((2,)), dma((2,)), dma((2,)), dma((4,)), dma, dma((ny,)), dma((ny,)), dma((ny,)),
            dma, dma((ny,)), dma((ny,)), dma((ny,)), dma((4,)),
        ],
        compiler_params=pltpu.CompilerParams(
            collective_id=0, has_side_effects=True, vmem_limit_bytes=40 * 1024 * 1024
        ),
    )(green_pair[:, :, :, 0], coulomb[0], offsets, green_retarded[:, :, 0], *consts)
    return dressed[:, :, None]


def solution(mesh):
    placed = (
        P(None, None, "wide", "cell", None, None),
        P("cell", None, None, None),
        P(None, "wide", "cell", None, None, None),
        P("cell", None),
    )
    return jax.shard_map(
        body,
        mesh=mesh,
        in_specs=placed,
        out_specs=P(None, "wide", "cell", None, None),
        check_vma=False,
    )
```

```python
import functools
import math

import jax
import jax.numpy as jnp
import numpy as np
from jax import lax
from jax.experimental import pallas as pl
from jax.experimental.pallas import tpu as pltpu
from jax.sharding import PartitionSpec as P

F32 = jnp.float32
BF16 = jnp.bfloat16
MESH = pl.DeviceIdType.MESH
WIDE_PARTS = (4, 4, 2)
LOCAL = 4


def split(value):
    high = value.astype(BF16)
    return high, (value - high.astype(F32)).astype(BF16)


def dot3(first, second, transposed=False):
    dims = (((1,), (1 if transposed else 0,)), ((), ()))
    multiply = functools.partial(lax.dot_general, dimension_numbers=dims, preferred_element_type=F32)
    return multiply(first[0], second[0]) + (multiply(first[0], second[1]) + multiply(first[1], second[0]))


def swap(value):
    tiles = value.reshape(value.shape[0] // 8, 8, value.shape[1])
    return jnp.concatenate([tiles[:, 4:], tiles[:, :4]], 1).reshape(value.shape)


def real_rows(shape):
    return lax.broadcasted_iota(jnp.int32, shape, 0) % 8 < 4


def tables(energies):
    period = 2 * energies
    angle = np.outer(np.arange(period), np.arange(energies)) % period * (2.0 * math.pi / period)

    def ordered(real_real, real_imag, imag_real, imag_imag):
        grid = np.array([[real_real, real_imag], [imag_real, imag_imag]])
        rows, columns = real_real.shape
        grid = grid.reshape(2, 2, rows // 4, 4, columns // 4, 4).transpose(2, 0, 3, 4, 1, 5)
        return grid.reshape(2 * rows, 2 * columns)

    cos, sin = np.cos(angle), np.sin(angle)
    scale = 1.0 / (period * energies)
    result = []
    for table in (ordered(cos, sin, -sin, cos), scale * ordered(cos.T, -sin.T, sin.T, cos.T)):
        table = table.astype(np.float32)
        high = table.astype(BF16)
        result += [high, (table - high.astype(np.float32)).astype(BF16)]
    return result


def kernel(
    green_in, coulomb_in, offsets_in, retarded_in, fwd_hi_in, fwd_lo_in, inv_hi_in, inv_lo_in, out,
    green, retarded, fwd_hi, fwd_lo, inv_hi, inv_lo, offsets,
    pack, pairs, lhat, psend, precv, below, above, vboth, vhi, vlo, sel, yy, zsend, srecv, qsend, sig, sigh,
    left_hi, left_lo, right_hi, right_lo,
    load_sem, local_sem, small_send, small_recv, send_sem, a_sem, p_sem, up_sem, down_sem, s_sem, q_sem, h_sem, fwd_sem,
):
    wide, cell = lax.axis_index("wide"), lax.axis_index("cell")
    cells = lax.axis_size("cell")
    nx, nh, nc = WIDE_PARTS
    ny = 2 * nh
    group = nx * nc
    plane = ny * group
    order = green.shape[-1]
    core, yh, x = wide % nc, wide // nc % nh, wide // (nc * nh)
    yl, z = cell % 2, cell // 2
    y = 2 * yh + yl
    place = (y * nx + x) * nc + core
    up, down = (wide, (cell + 2) % cells), (wide, (cell + cells - 2) % cells)
    has_up, has_down = z < cells // 2 - 1, z > 0
    partner = (wide, cell + 1 - 2 * yl)

    def rows8(index):
        return pl.ds(pl.multiple_of(8 * index, 8), 8)

    def rise(g):
        k = ny - 1 - g
        return jnp.where(k % 2 == 1, (k + 1) // 2, (ny - k // 2) % ny)

    columns = [((x + h // nc) % nx, (core + h % nc) % nc) for h in range(group)]
    columns = [(x2 * nh * nc + c2, x2 * nc + c2) for x2, c2 in columns]

    def each_peer(act):
        def at(g, first):
            y2 = y + rise(g)
            y2 = jnp.where(y2 >= ny, y2 - ny, y2)
            yh2 = y2 // 2
            act(g, [(yh2 * nc + w, y2 * group + p) for w, p in columns[first:]], y2 - 2 * yh2)

        def step(g, carry):
            at(g, 0)
            return carry

        lax.fori_loop(0, ny - 1, step, 0)
        at(ny - 1, 1)

    def remote(src, dst, send, recv, device):
        return pltpu.make_async_remote_copy(
            src_ref=src, dst_ref=dst, send_sem=send, recv_sem=recv, device_id=device, device_id_type=MESH
        )

    def await_bytes(like, sem):
        pltpu.make_async_copy(like, like, sem).wait()

    def chunk(g):
        y0 = (y + ny - rise(g)) % ny
        return pl.ds(pl.multiple_of(y0 * (8 * group), 8 * group), 8 * group)

    def exchange(source, target, send, recv_of):
        def act(g, devices, yl2):
            for wide2, place2 in devices:
                remote(source(place2), target, send, recv_of(g), (wide2, 2 * z + yl2)).start()

        each_peer(act)

    others = pl.ds(0, 8 * plane - 8)

    loads = [
        pltpu.make_async_copy(src, dst, load_sem.at[i])
        for i, (src, dst) in enumerate((
            (green_in, green), (coulomb_in, vboth.at[yl]), (offsets_in, offsets), (fwd_hi_in, fwd_hi),
            (fwd_lo_in, fwd_lo), (inv_hi_in, inv_hi), (inv_lo_in, inv_lo), (retarded_in, retarded),
        ))
    ]
    for load in loads:
        load.start()

    barrier = pltpu.get_barrier_semaphore()

    def greet(g, devices, yl2):
        for wide2, place2 in devices:
            pl.semaphore_signal(barrier, inc=1, device_id=(wide2, 2 * z + yl2), device_id_type=MESH)

    each_peer(greet)
    for device, there in ((up, has_up), (down, has_down)):
        @pl.when(there)
        def _():
            pl.semaphore_signal(barrier, inc=1, device_id=device, device_id_type=MESH)

    near_receives = jnp.where(yl == 0, has_down, has_up)
    near_sends = jnp.where(yl == 0, has_up, has_down)
    loads[0].wait()

    for i in range(2):
        for pair in range(2):
            for part in range(2):
                for e in range(LOCAL):
                    pack[i, pair, pl.ds(4 * part + e, plane, stride=8), :] = green[
                        pair, part, e, i * plane : (i + 1) * plane, :
                    ]
    pl.semaphore_wait(barrier, plane - 1 + jnp.where(has_up, 1, 0) + jnp.where(has_down, 1, 0))

    own = []
    for i in range(2):
        exchange(
            lambda place2: pack.at[i, :, rows8(place2), :], pairs.at[i, :, yl, rows8(wide), :],
            send_sem.at[0], lambda g: a_sem.at[i],
        )
        own.append(pltpu.make_async_copy(
            pack.at[i, :, rows8(place), :], pairs.at[i, :, yl, rows8(wide), :], local_sem.at[i]
        ))
        own[i].start()
    for load in loads[1:]:
        load.wait()
    for slot in range(2):
        sel[yl, slot] = jnp.where(jnp.full((8, order), offsets[0, slot], jnp.int32) != 0, 1.0, 0.0)
    coulomb_copy = remote(vboth.at[yl], vboth.at[yl], small_send.at[0], small_recv.at[0], partner)
    coulomb_copy.start()
    masks_copy = remote(sel.at[yl], sel.at[yl], small_send.at[1], small_recv.at[1], partner)
    masks_copy.start()

    @pl.when(jnp.logical_not(has_down))
    def _():
        below[...] = jnp.zeros_like(below)

    @pl.when(jnp.logical_not(has_up))
    def _():
        above[...] = jnp.zeros_like(above)

    @pl.when(jnp.logical_not(near_receives))
    def _():
        sigh[...] = jnp.zeros_like(sigh)

    @pl.when(yl == 0)
    def _():
        sig[0] = jnp.zeros(sig.shape[1:], F32)

    tile = min(128, fwd_hi.shape[0])
    for i in range(2):
        own[i].wait()
        await_bytes(pack.at[i, :, others, :], a_sem.at[i])

        def transform(r, carry):
            lesser, greater = pairs[i, 0, r], pairs[i, 1, r]
            conjugate = jnp.where(real_rows(greater.shape), greater, -greater)
            rhs = split(jnp.concatenate([lesser, conjugate], 1))
            for m in range(fwd_hi.shape[0] // tile):
                rows = slice(m * tile, (m + 1) * tile)
                both = dot3((fwd_hi[rows], fwd_lo[rows]), rhs)
                first, second = both[:, :order], both[:, order:]
                lhat[i, r, rows, :] = first
                same, cross = first * second, first * swap(second)
                psend[i, r, rows, :] = jnp.where(real_rows(same.shape), same + swap(same), cross - swap(cross))
            return carry

        lax.fori_loop(0, 2, transform, 0)
        exchange(
            lambda place2: psend.at[i, :, rows8(place2), :], precv.at[i, :, rows8(place), :],
            send_sem.at[1], lambda g: p_sem.at[i, g],
        )
        pltpu.make_async_copy(
            psend.at[i, :, rows8(place), :], precv.at[i, :, rows8(place), :], p_sem.at[i, ny - 1]
        ).start()

    coulomb_copy.wait()
    masks_copy.wait()
    for r in range(2):
        for slot in range(2):
            high, low = split(vboth[r, slot])
            vhi[r, :, slot * order : (slot + 1) * order] = high
            vlo[r, :, slot * order : (slot + 1) * order] = low

    def prepare(e, carry):
        for slot in range(2):
            at = 2 * e + slot
            (rh, rl), (ih, il) = split(retarded[0, e, slot]), split(retarded[1, e, slot])
            for left, right, real, imag in ((left_hi, right_hi, rh, ih), (left_lo, right_lo, rl, il)):
                left[at, :, :order] = real
                left[at, :, order:] = imag
                right[at, :order, :order] = real
                right[at, :order, order:] = -imag
                right[at, order:, :order] = imag
                right[at, order:, order:] = real
        return carry

    lax.fori_loop(0, LOCAL, prepare, 0)

    for i in range(2):
        def forward(g, carry):
            rows = chunk(g)
            await_bytes(precv.at[i, :, rows, :], p_sem.at[i, g])

            @pl.when(has_up)
            def _():
                remote(precv.at[i, 1, rows, :], below.at[i, rows, :], fwd_sem.at[0], up_sem.at[i, g], up).start()

            @pl.when(has_down)
            def _():
                remote(precv.at[i, 0, rows, :], above.at[i, rows, :], fwd_sem.at[1], down_sem.at[i, g], down).start()

            return carry

        lax.fori_loop(0, ny, forward, 0)

    full = 8 * plane
    part_rows = min(256, full)
    for i in range(2):
        def arrive(g, carry):
            rows = chunk(g)

            @pl.when(has_down)
            def _():
                await_bytes(below.at[i, rows, :], up_sem.at[i, g])

            @pl.when(has_up)
            def _():
                await_bytes(above.at[i, rows, :], down_sem.at[i, g])

            return carry

        lax.fori_loop(0, ny, arrive, 0)

        def from_right(m, carry):
            rows = pl.ds(pl.multiple_of(m * part_rows, part_rows), part_rows)
            lower, even, odd, upper = below[i, rows, :], precv[i, 0, rows, :], precv[i, 1, rows, :], above[i, rows, :]
            first = jnp.where(sel[1, 0, 0:1, :] > 0.5, even, odd)
            second = jnp.where(sel[1, 1, 0:1, :] > 0.5, upper, odd)
            for r, slot, value in ((1, 0, first), (1, 1, second), (0, 0, lower), (0, 1, odd)):
                block = slice(slot * order, (slot + 1) * order)
                yy[r, slot, i, rows, :] = dot3(split(value), (vhi[r, :, block], vlo[r, :, block]), True)
            return carry

        lax.fori_loop(0, full // part_rows, from_right, 0)

    own = {}
    for r in (1, 0):
        def from_left(t, carry):
            sides = []
            for part in range(2):
                sides.append(jnp.concatenate(
                    [yy[r, slot, i, pl.ds(4 * part + t, plane, stride=8), :] for slot in range(2) for i in range(2)], 0
                ))
            done = dot3((vhi[r], vlo[r]), split(jnp.concatenate(sides, 1)))
            for part in range(2):
                for i in range(2):
                    zsend[r, i, pl.ds(4 * part + t, plane, stride=8), :] = done[
                        i * plane : (i + 1) * plane, part * order : (part + 1) * order
                    ]
            return carry

        for t in range(LOCAL):
            from_left(t, 0)
        exchange(
            lambda place2: zsend.at[r, :, rows8(place2), :], srecv.at[r, :, rows8(place), :],
            send_sem.at[2], lambda g: s_sem.at[r],
        )
        own[r] = pltpu.make_async_copy(
            zsend.at[r, :, rows8(place), :], srecv.at[r, :, rows8(place), :], local_sem.at[2 + r]
        )
        own[r].start()

    for r in (1, 0):
        own[r].wait()
        await_bytes(zsend.at[r, :, others, :], s_sem.at[r])
        sides = []
        for i in range(2):
            first, second = lhat[i, r], srecv[r, i]
            same, cross = first * second, first * swap(second)
            sides.append(jnp.where(real_rows(same.shape), same - swap(same), cross + swap(cross)))
        rhs = split(jnp.concatenate(sides, 1))
        tile = min(128, inv_hi.shape[0])
        for m in range(inv_hi.shape[0] // tile):
            rows = slice(m * tile, (m + 1) * tile)
            done = dot3((inv_hi[rows], inv_lo[rows]), rhs)
            for i in range(2):
                qsend[r, i, rows, :] = done[:, i * order : (i + 1) * order]

        def send_sigma(g, devices, yl2):
            def send():
                for wide2, place2 in devices:
                    remote(
                        qsend.at[r, :, rows8(wide2), :], sig.at[r, :, rows8(place), :],
                        send_sem.at[3 + r], q_sem.at[r, g], (wide2, 2 * z + yl2),
                    ).start()

            if r == 1:
                send()
            else:
                pl.when(yl2 == 1)(send)

        each_peer(send_sigma)

        def keep():
            pltpu.make_async_copy(
                qsend.at[r, :, rows8(wide), :], sig.at[r, :, rows8(place), :], q_sem.at[r, ny - 1]
            ).start()

        if r == 1:
            keep()
        else:
            pl.when(yl == 1)(keep)

    for r, parity, device in ((1, 0, up), (0, 1, down)):
        def spread(g, carry):
            rows = chunk(g)
            await_bytes(sig.at[r, :, rows, :], q_sem.at[r, g])

            @pl.when(jnp.logical_and(near_sends, yl == parity))
            def _():
                remote(sig.at[r, :, rows, :], sigh.at[:, rows, :], fwd_sem.at[2], h_sem.at[g], device).start()

            return carry

        if r == 1:
            lax.fori_loop(0, ny, spread, 0)
        else:
            @pl.when(yl == 1)
            def _():
                lax.fori_loop(0, ny, spread, 0)

    def term(at, real, imag):
        left = dot3(
            (left_hi[at], left_lo[at]),
            split(jnp.concatenate([jnp.concatenate([real, imag], 1), jnp.concatenate([-imag, real], 1)], 0)),
        )
        return dot3(split(left), (right_hi[at], right_lo[at]), True)

    def block(ref, e, part, *lead):
        return jnp.concatenate(
            [ref[(*lead, i, pl.ds(4 * part + e, plane, stride=8), slice(None))] for i in range(2)], 0
        )

    odd_cell = jnp.full((8, order), yl, jnp.int32) == 1
    take_near = jnp.logical_and(odd_cell, sel[yl, 0] > 0.5)[0:1]
    take_far = jnp.logical_or(jnp.logical_not(odd_cell), sel[yl, 1] > 0.5)[0:1]
    for e in range(LOCAL):
        real, imag = (jnp.where(take_near, block(sig, e, part, 0), block(sig, e, part, 1)) for part in range(2))
        done = term(2 * e + 1 - yl, real, imag)
        out[0, e] = done[:, :order]
        out[1, e] = done[:, order:]

    def arrive_far(g, carry):
        await_bytes(sigh.at[:, chunk(g), :], h_sem.at[g])
        return carry

    @pl.when(near_receives)
    def _():
        lax.fori_loop(0, ny, arrive_far, 0)

    for e in range(LOCAL):
        real, imag = (jnp.where(take_far, block(sigh, e, part), block(sig, e, part, 1)) for part in range(2))
        done = term(2 * e + yl, real, imag)
        out[0, e] += done[:, :order]
        out[1, e] += done[:, order:]

    for phase, ref in enumerate((pack, psend, zsend)):
        await_bytes(ref.at[:, :, others, :], send_sem.at[phase])
    await_bytes(sig.at[1, :, others, :], send_sem.at[4])

    @pl.when(yl == 0)
    def _():
        await_bytes(sig.at[0, :, pl.ds(0, 4 * plane), :], send_sem.at[3])

    @pl.when(yl == 1)
    def _():
        await_bytes(sig.at[0, :, pl.ds(0, 4 * plane - 8), :], send_sem.at[3])

    @pl.when(has_up)
    def _():
        await_bytes(below, fwd_sem.at[0])

    @pl.when(has_down)
    def _():
        await_bytes(above, fwd_sem.at[1])

    @pl.when(near_sends)
    def _():
        await_bytes(sigh, fwd_sem.at[2])


def body(green_pair, coulomb, green_retarded, offsets):
    nx, nh, nc = WIDE_PARTS
    ny, plane = 2 * nh, 2 * nx * nh * nc
    order, local = green_pair.shape[-1], green_pair.shape[2]
    energies = local * nx * nh * nc
    full = 8 * plane
    consts = [jnp.asarray(value) for value in tables(energies)]
    hbm = pl.BlockSpec(memory_space=pltpu.HBM)
    arguments = (green_pair[:, :, :, 0], coulomb[0], offsets, green_retarded[:, :, 0], *consts)
    dma = pltpu.SemaphoreType.DMA
    dressed = pl.pallas_call(
        kernel,
        out_shape=jax.ShapeDtypeStruct((2, local, order, order), F32),
        in_specs=[hbm] * len(arguments),
        out_specs=pl.BlockSpec(memory_space=pltpu.VMEM),
        scratch_shapes=[
            pltpu.VMEM(arguments[0].shape, F32),
            pltpu.VMEM(arguments[3].shape, F32),
            *(pltpu.VMEM(value.shape, BF16) for value in consts),
            pltpu.SMEM((1, 2), jnp.int32),
            pltpu.VMEM((2, 2, full, order), F32),
            pltpu.VMEM((2, 2, 2, full // 2, order), F32),
            pltpu.VMEM((2, 2, full, order), F32),
            pltpu.VMEM((2, 2, full, order), F32),
            pltpu.VMEM((2, 2, full, order), F32),
            pltpu.VMEM((2, full, order), F32),
            pltpu.VMEM((2, full, order), F32),
            pltpu.VMEM((2, 2, order, order), F32),
            pltpu.VMEM((2, order, 2 * order), BF16),
            pltpu.VMEM((2, order, 2 * order), BF16),
            pltpu.VMEM((2, 2, 8, order), F32),
            pltpu.VMEM((2, 2, 2, full, order), F32),
            pltpu.VMEM((2, 2, full, order), F32),
            pltpu.VMEM((2, 2, full, order), F32),
            pltpu.VMEM((2, 2, full // 2, order), F32),
            pltpu.VMEM((2, 2, full, order), F32),
            pltpu.VMEM((2, full, order), F32),
            *[pltpu.VMEM((2 * local, order, 2 * order), BF16)] * 2,
            *[pltpu.VMEM((2 * local, 2 * order, 2 * order), BF16)] * 2,
            dma((8,)), dma((4,)), dma((2,)), dma((2,)), dma((5,)), dma((2,)), dma((2, ny)), dma((2, ny)), dma((2, ny)),
            dma((2,)), dma((2, ny)), dma((ny,)), dma((3,)),
        ],
        compiler_params=pltpu.CompilerParams(
            collective_id=0, has_side_effects=True, vmem_limit_bytes=60 * 1024 * 1024
        ),
    )(*arguments)
    return dressed[:, :, None]


def solution(mesh):
    placed = (
        P(None, None, "wide", "cell", None, None),
        P("cell", None, None, None),
        P(None, "wide", "cell", None, None, None),
        P("cell", None),
    )
    return jax.shard_map(
        body,
        mesh=mesh,
        in_specs=placed,
        out_specs=P(None, "wide", "cell", None, None),
        check_vma=False,
    )
```

```python
import functools
import math

import jax
import jax.numpy as jnp
import numpy as np
from jax import lax
from jax.experimental import pallas as pl
from jax.experimental.pallas import tpu as pltpu
from jax.sharding import PartitionSpec as P

F32 = jnp.float32
BF16 = jnp.bfloat16
MESH = pl.DeviceIdType.MESH
WIDE_PARTS = (4, 4, 2)
LOCAL = 4


def split(value):
    high = value.astype(BF16)
    return high, (value - high.astype(F32)).astype(BF16)


def dot3(first, second, transposed=False):
    dims = (((1,), (1 if transposed else 0,)), ((), ()))
    multiply = functools.partial(lax.dot_general, dimension_numbers=dims, preferred_element_type=F32)
    return multiply(first[0], second[0]) + (multiply(first[0], second[1]) + multiply(first[1], second[0]))


def swap(value):
    tiles = value.reshape(value.shape[0] // 8, 8, value.shape[1])
    return jnp.concatenate([tiles[:, 4:], tiles[:, :4]], 1).reshape(value.shape)


def real_rows(shape):
    return lax.broadcasted_iota(jnp.int32, shape, 0) % 8 < 4


def tables(energies):
    period = 2 * energies
    angle = np.outer(np.arange(period), np.arange(energies)) % period * (2.0 * math.pi / period)

    def ordered(real_real, real_imag, imag_real, imag_imag):
        grid = np.array([[real_real, real_imag], [imag_real, imag_imag]])
        rows, columns = real_real.shape
        grid = grid.reshape(2, 2, rows // 4, 4, columns // 4, 4).transpose(2, 0, 3, 4, 1, 5)
        return grid.reshape(2 * rows, 2 * columns)

    cos, sin = np.cos(angle), np.sin(angle)
    scale = 1.0 / (period * energies)
    result = []
    for table in (ordered(cos, sin, -sin, cos), scale * ordered(cos.T, -sin.T, sin.T, cos.T)):
        table = table.astype(np.float32)
        high = table.astype(BF16)
        result += [high, (table - high.astype(np.float32)).astype(BF16)]
    return result


def kernel(
    green_in, coulomb_in, offsets_in, retarded_in, fwd_hi_in, fwd_lo_in, inv_hi_in, inv_lo_in, out,
    green, retarded, fwd_hi, fwd_lo, inv_hi, inv_lo, offsets,
    pack, pairs, lhat, psend, precv, below, above, vboth, vhi, vlo, sel, yy, zsend, srecv, qsend, qhalo, xsend, sig,
    left_hi, left_lo, right_hi, right_lo,
    load_sem, local_sem, small_send, small_recv, send_sem, a_sem, p_sem, up_sem, down_sem, s_sem, q_sem, h_sem, x_sem, halo_sem, fwd_sem,
):
    wide, cell = lax.axis_index("wide"), lax.axis_index("cell")
    cells = lax.axis_size("cell")
    nx, nh, nc = WIDE_PARTS
    ny = 2 * nh
    group = nx * nc
    plane = ny * group
    order = green.shape[-1]
    core, yh, x = wide % nc, wide // nc % nh, wide // (nc * nh)
    yl, z = cell % 2, cell // 2
    y = 2 * yh + yl
    place = (y * nx + x) * nc + core
    up, down = (wide, (cell + 2) % cells), (wide, (cell + cells - 2) % cells)
    has_up, has_down = z < cells // 2 - 1, z > 0
    partner = (wide, cell + 1 - 2 * yl)

    def rows8(index):
        return pl.ds(pl.multiple_of(8 * index, 8), 8)

    def rise(g):
        k = ny - 1 - g
        return jnp.where(k % 2 == 1, (k + 1) // 2, (ny - k // 2) % ny)

    columns = [((x + h // nc) % nx, (core + h % nc) % nc) for h in range(group)]
    columns = [(x2 * nh * nc + c2, x2 * nc + c2) for x2, c2 in columns]

    def each_peer(act):
        def at(g, first):
            y2 = y + rise(g)
            y2 = jnp.where(y2 >= ny, y2 - ny, y2)
            yh2 = y2 // 2
            act(g, [(yh2 * nc + w, y2 * group + p) for w, p in columns[first:]], y2 - 2 * yh2)

        def step(g, carry):
            at(g, 0)
            return carry

        lax.fori_loop(0, ny - 1, step, 0)
        at(ny - 1, 1)

    def remote(src, dst, send, recv, device):
        return pltpu.make_async_remote_copy(
            src_ref=src, dst_ref=dst, send_sem=send, recv_sem=recv, device_id=device, device_id_type=MESH
        )

    def await_bytes(like, sem):
        pltpu.make_async_copy(like, like, sem).wait()

    def chunk(g):
        y0 = (y + ny - rise(g)) % ny
        return pl.ds(pl.multiple_of(y0 * (8 * group), 8 * group), 8 * group)

    def exchange(source, target, send, recv_of):
        def act(g, devices, yl2):
            for wide2, place2 in devices:
                remote(source(place2), target, send, recv_of(g), (wide2, 2 * z + yl2)).start()

        each_peer(act)

    others = pl.ds(0, 8 * plane - 8)

    loads = [
        pltpu.make_async_copy(src, dst, load_sem.at[i])
        for i, (src, dst) in enumerate((
            (green_in, green), (coulomb_in, vboth.at[yl]), (offsets_in, offsets), (fwd_hi_in, fwd_hi),
            (fwd_lo_in, fwd_lo), (inv_hi_in, inv_hi), (inv_lo_in, inv_lo), (retarded_in, retarded),
        ))
    ]
    for load in loads:
        load.start()

    barrier = pltpu.get_barrier_semaphore()

    def greet(g, devices, yl2):
        for wide2, place2 in devices:
            pl.semaphore_signal(barrier, inc=1, device_id=(wide2, 2 * z + yl2), device_id_type=MESH)

    each_peer(greet)
    for device, there in ((up, has_up), (down, has_down)):
        @pl.when(there)
        def _():
            pl.semaphore_signal(barrier, inc=1, device_id=device, device_id_type=MESH)

    even_sends, even_receives = jnp.logical_and(yl == 0, has_up), jnp.logical_and(yl == 0, has_down)
    loads[0].wait()

    for i in range(2):
        for pair in range(2):
            for part in range(2):
                for e in range(LOCAL):
                    pack[i, pair, pl.ds(4 * part + e, plane, stride=8), :] = green[
                        pair, part, e, i * plane : (i + 1) * plane, :
                    ]
    pl.semaphore_wait(barrier, plane - 1 + jnp.where(has_up, 1, 0) + jnp.where(has_down, 1, 0))

    own = []
    for i in range(2):
        exchange(
            lambda place2: pack.at[i, :, rows8(place2), :], pairs.at[i, :, yl, rows8(wide), :],
            send_sem.at[0], lambda g: a_sem.at[i],
        )
        own.append(pltpu.make_async_copy(
            pack.at[i, :, rows8(place), :], pairs.at[i, :, yl, rows8(wide), :], local_sem.at[i]
        ))
        own[i].start()
    for load in loads[1:]:
        load.wait()
    for slot in range(2):
        sel[yl, slot] = jnp.where(jnp.full((8, order), offsets[0, slot], jnp.int32) != 0, 1.0, 0.0)
    coulomb_copy = remote(vboth.at[yl], vboth.at[yl], small_send.at[0], small_recv.at[0], partner)
    coulomb_copy.start()
    masks_copy = remote(sel.at[yl], sel.at[yl], small_send.at[1], small_recv.at[1], partner)
    masks_copy.start()

    @pl.when(jnp.logical_not(has_down))
    def _():
        below[...] = jnp.zeros_like(below)

    @pl.when(jnp.logical_not(has_up))
    def _():
        above[...] = jnp.zeros_like(above)
        qhalo[...] = jnp.zeros_like(qhalo)

    @pl.when(jnp.logical_and(yl == 0, jnp.logical_not(has_down)))
    def _():
        sig[0] = jnp.zeros(sig.shape[1:], F32)

    tile = min(128, fwd_hi.shape[0])
    for i in range(2):
        own[i].wait()
        await_bytes(pack.at[i, :, others, :], a_sem.at[i])

        def transform(r, carry):
            lesser, greater = pairs[i, 0, r], pairs[i, 1, r]
            conjugate = jnp.where(real_rows(greater.shape), greater, -greater)
            rhs = split(jnp.concatenate([lesser, conjugate], 1))
            for m in range(fwd_hi.shape[0] // tile):
                rows = slice(m * tile, (m + 1) * tile)
                both = dot3((fwd_hi[rows], fwd_lo[rows]), rhs)
                first, second = both[:, :order], both[:, order:]
                lhat[i, r, rows, :] = first
                same, cross = first * second, first * swap(second)
                psend[i, r, rows, :] = jnp.where(real_rows(same.shape), same + swap(same), cross - swap(cross))
            return carry

        lax.fori_loop(0, 2, transform, 0)
        exchange(
            lambda place2: psend.at[i, :, rows8(place2), :], precv.at[i, :, rows8(place), :],
            send_sem.at[1], lambda g: p_sem.at[i, g],
        )
        pltpu.make_async_copy(
            psend.at[i, :, rows8(place), :], precv.at[i, :, rows8(place), :], p_sem.at[i, ny - 1]
        ).start()

    coulomb_copy.wait()
    masks_copy.wait()
    for r in range(2):
        for slot in range(2):
            high, low = split(vboth[r, slot])
            vhi[r, :, slot * order : (slot + 1) * order] = high
            vlo[r, :, slot * order : (slot + 1) * order] = low

    def prepare(e, carry):
        for slot in range(2):
            at = 2 * e + slot
            (rh, rl), (ih, il) = split(retarded[0, e, slot]), split(retarded[1, e, slot])
            for left, right, real, imag in ((left_hi, right_hi, rh, ih), (left_lo, right_lo, rl, il)):
                left[at, :, :order] = real
                left[at, :, order:] = imag
                right[at, :order, :order] = real
                right[at, :order, order:] = -imag
                right[at, order:, :order] = imag
                right[at, order:, order:] = real
        return carry

    lax.fori_loop(0, LOCAL, prepare, 0)

    for i in range(2):
        def forward(g, carry):
            rows = chunk(g)
            await_bytes(precv.at[i, :, rows, :], p_sem.at[i, g])

            @pl.when(has_up)
            def _():
                remote(precv.at[i, 1, rows, :], below.at[i, rows, :], fwd_sem.at[0], up_sem.at[i, g], up).start()

            @pl.when(has_down)
            def _():
                remote(precv.at[i, 0, rows, :], above.at[i, rows, :], fwd_sem.at[1], down_sem.at[i, g], down).start()

            return carry

        lax.fori_loop(0, ny, forward, 0)

    full = 8 * plane
    part_rows = min(256, full)
    for i in range(2):
        def arrive(g, carry):
            rows = chunk(g)

            @pl.when(has_down)
            def _():
                await_bytes(below.at[i, rows, :], up_sem.at[i, g])

            @pl.when(has_up)
            def _():
                await_bytes(above.at[i, rows, :], down_sem.at[i, g])

            return carry

        lax.fori_loop(0, ny, arrive, 0)

        def from_right(m, carry):
            rows = pl.ds(pl.multiple_of(m * part_rows, part_rows), part_rows)
            lower, even, odd, upper = below[i, rows, :], precv[i, 0, rows, :], precv[i, 1, rows, :], above[i, rows, :]
            first = jnp.where(sel[1, 0, 0:1, :] > 0.5, even, odd)
            second = jnp.where(sel[1, 1, 0:1, :] > 0.5, upper, odd)
            for r, slot, value in ((1, 0, first), (1, 1, second), (0, 0, lower), (0, 1, odd)):
                block = slice(slot * order, (slot + 1) * order)
                yy[r, slot, i, rows, :] = dot3(split(value), (vhi[r, :, block], vlo[r, :, block]), True)
            return carry

        lax.fori_loop(0, full // part_rows, from_right, 0)

    own = {}
    for r in (1, 0):
        def from_left(t, carry):
            sides = []
            for part in range(2):
                sides.append(jnp.concatenate(
                    [yy[r, slot, i, pl.ds(4 * part + t, plane, stride=8), :] for slot in range(2) for i in range(2)], 0
                ))
            done = dot3((vhi[r], vlo[r]), split(jnp.concatenate(sides, 1)))
            for part in range(2):
                for i in range(2):
                    zsend[r, i, pl.ds(4 * part + t, plane, stride=8), :] = done[
                        i * plane : (i + 1) * plane, part * order : (part + 1) * order
                    ]
            return carry

        for t in range(LOCAL):
            from_left(t, 0)
        exchange(
            lambda place2: zsend.at[r, :, rows8(place2), :], srecv.at[r, :, rows8(place), :],
            send_sem.at[2], lambda g: s_sem.at[r],
        )
        own[r] = pltpu.make_async_copy(
            zsend.at[r, :, rows8(place), :], srecv.at[r, :, rows8(place), :], local_sem.at[2 + r]
        )
        own[r].start()

    def self_energy(r):
        own[r].wait()
        await_bytes(zsend.at[r, :, others, :], s_sem.at[r])
        sides = []
        for i in range(2):
            first, second = lhat[i, r], srecv[r, i]
            same, cross = first * second, first * swap(second)
            sides.append(jnp.where(real_rows(same.shape), same - swap(same), cross + swap(cross)))
        rhs = split(jnp.concatenate(sides, 1))
        tile = min(128, inv_hi.shape[0])
        for m in range(inv_hi.shape[0] // tile):
            rows = slice(m * tile, (m + 1) * tile)
            done = dot3((inv_hi[rows], inv_lo[rows]), rhs)
            for i in range(2):
                qsend[r, i, rows, :] = done[:, i * order : (i + 1) * order]

    def send_sigma(source, slot, parity, send, recv_of):
        def act(g, devices, yl2):
            @pl.when(yl2 == parity)
            def _():
                for wide2, place2 in devices:
                    remote(
                        source.at[:, rows8(wide2), :], sig.at[slot, :, rows8(place), :],
                        send, recv_of(g), (wide2, 2 * z + parity),
                    ).start()

        each_peer(act)

        @pl.when(yl == parity)
        def _():
            pltpu.make_async_copy(
                source.at[:, rows8(wide), :], sig.at[slot, :, rows8(place), :], recv_of(ny - 1)
            ).start()

    self_energy(1)
    send_sigma(qsend.at[1], 1, 0, send_sem.at[3], lambda g: q_sem.at[g])
    self_energy(0)

    @pl.when(has_down)
    def _():
        remote(qsend.at[0], qhalo, fwd_sem.at[3], halo_sem, down).start()

    xsend[0] = jnp.where(sel[1, 0, 0:1, :] > 0.5, qsend[0], qsend[1])
    send_sigma(xsend.at[0], 0, 1, send_sem.at[4], lambda g: x_sem.at[0])

    def spread(g, carry):
        rows = chunk(g)
        await_bytes(sig.at[1, :, rows, :], q_sem.at[g])

        @pl.when(has_up)
        def _():
            remote(sig.at[1, :, rows, :], sig.at[0, :, rows, :], fwd_sem.at[2], h_sem.at[g], up).start()

        return carry

    @pl.when(yl == 0)
    def _():
        lax.fori_loop(0, ny, spread, 0)

    @pl.when(has_up)
    def _():
        await_bytes(qhalo, halo_sem)

    xsend[1] = jnp.where(sel[1, 1, 0:1, :] > 0.5, qhalo[...], qsend[1])
    send_sigma(xsend.at[1], 1, 1, send_sem.at[5], lambda g: x_sem.at[1])

    def term(at, real, imag):
        left = dot3(
            (left_hi[at], left_lo[at]),
            split(jnp.concatenate([jnp.concatenate([real, imag], 1), jnp.concatenate([-imag, real], 1)], 0)),
        )
        return dot3(split(left), (right_hi[at], right_lo[at]), True)

    def dress(e, slot):
        real, imag = (
            jnp.concatenate([sig[slot, i, pl.ds(4 * part + e, plane, stride=8), :] for i in range(2)], 0)
            for part in range(2)
        )
        return term(2 * e + slot, real, imag)

    @pl.when(yl == 1)
    def _():
        await_bytes(sig.at[0], x_sem.at[0])

    for e in range(LOCAL):
        done = dress(e, 1 - yl)
        out[0, e] = done[:, :order]
        out[1, e] = done[:, order:]

    @pl.when(yl == 1)
    def _():
        await_bytes(sig.at[1], x_sem.at[1])

    def arrive_far(g, carry):
        await_bytes(sig.at[0, :, chunk(g), :], h_sem.at[g])
        return carry

    @pl.when(even_receives)
    def _():
        lax.fori_loop(0, ny, arrive_far, 0)

    for e in range(LOCAL):
        done = dress(e, yl)
        out[0, e] += done[:, :order]
        out[1, e] += done[:, order:]

    for phase, ref in enumerate((pack, psend, zsend)):
        await_bytes(ref.at[:, :, others, :], send_sem.at[phase])
    for parity in range(2):
        @pl.when(yl == parity)
        def _():
            for phase in (3, 4, 5):
                fewer = 8 if (phase == 3) == (parity == 0) else 0
                await_bytes(sig.at[0, :, pl.ds(0, 4 * plane - fewer), :], send_sem.at[phase])

    @pl.when(has_up)
    def _():
        await_bytes(below, fwd_sem.at[0])

    @pl.when(has_down)
    def _():
        await_bytes(above, fwd_sem.at[1])
        await_bytes(qhalo, fwd_sem.at[3])

    @pl.when(even_sends)
    def _():
        await_bytes(sig.at[0], fwd_sem.at[2])


def body(green_pair, coulomb, green_retarded, offsets):
    nx, nh, nc = WIDE_PARTS
    ny, plane = 2 * nh, 2 * nx * nh * nc
    order, local = green_pair.shape[-1], green_pair.shape[2]
    energies = local * nx * nh * nc
    full = 8 * plane
    consts = [jnp.asarray(value) for value in tables(energies)]
    hbm = pl.BlockSpec(memory_space=pltpu.HBM)
    arguments = (green_pair[:, :, :, 0], coulomb[0], offsets, green_retarded[:, :, 0], *consts)
    dma = pltpu.SemaphoreType.DMA
    dressed = pl.pallas_call(
        kernel,
        out_shape=jax.ShapeDtypeStruct((2, local, order, order), F32),
        in_specs=[hbm] * len(arguments),
        out_specs=pl.BlockSpec(memory_space=pltpu.VMEM),
        scratch_shapes=[
            pltpu.VMEM(arguments[0].shape, F32),
            pltpu.VMEM(arguments[3].shape, F32),
            *(pltpu.VMEM(value.shape, BF16) for value in consts),
            pltpu.SMEM((1, 2), jnp.int32),
            pltpu.VMEM((2, 2, full, order), F32),
            pltpu.VMEM((2, 2, 2, full // 2, order), F32),
            pltpu.VMEM((2, 2, full, order), F32),
            pltpu.VMEM((2, 2, full, order), F32),
            pltpu.VMEM((2, 2, full, order), F32),
            pltpu.VMEM((2, full, order), F32),
            pltpu.VMEM((2, full, order), F32),
            pltpu.VMEM((2, 2, order, order), F32),
            pltpu.VMEM((2, order, 2 * order), BF16),
            pltpu.VMEM((2, order, 2 * order), BF16),
            pltpu.VMEM((2, 2, 8, order), F32),
            pltpu.VMEM((2, 2, 2, full, order), F32),
            pltpu.VMEM((2, 2, full, order), F32),
            pltpu.VMEM((2, 2, full, order), F32),
            pltpu.VMEM((2, 2, full // 2, order), F32),
            pltpu.VMEM((2, full // 2, order), F32),
            pltpu.VMEM((2, 2, full // 2, order), F32),
            pltpu.VMEM((2, 2, full, order), F32),
            *[pltpu.VMEM((2 * local, order, 2 * order), BF16)] * 2,
            *[pltpu.VMEM((2 * local, 2 * order, 2 * order), BF16)] * 2,
            dma((8,)), dma((4,)), dma((2,)), dma((2,)), dma((6,)), dma((2,)), dma((2, ny)), dma((2, ny)), dma((2, ny)),
            dma((2,)), dma((ny,)), dma((ny,)), dma((2,)), dma, dma((4,)),
        ],
        compiler_params=pltpu.CompilerParams(
            collective_id=0, has_side_effects=True, vmem_limit_bytes=60 * 1024 * 1024
        ),
    )(*arguments)
    return dressed[:, :, None]


def solution(mesh):
    placed = (
        P(None, None, "wide", "cell", None, None),
        P("cell", None, None, None),
        P(None, "wide", "cell", None, None, None),
        P("cell", None),
    )
    return jax.shard_map(
        body,
        mesh=mesh,
        in_specs=placed,
        out_specs=P(None, "wide", "cell", None, None),
        check_vma=False,
    )
```

```python
import functools
import math

import jax
import jax.numpy as jnp
import numpy as np
from jax import lax
from jax.experimental import pallas as pl
from jax.experimental.pallas import tpu as pltpu
from jax.sharding import PartitionSpec as P

F32 = jnp.float32
BF16 = jnp.bfloat16
MESH = pl.DeviceIdType.MESH
WIDE_PARTS = (4, 4, 2)
LOCAL = 4


def split(value):
    high = value.astype(BF16)
    return high, (value - high.astype(F32)).astype(BF16)


def dot3(first, second, transposed=False):
    dims = (((1,), (1 if transposed else 0,)), ((), ()))
    multiply = functools.partial(lax.dot_general, dimension_numbers=dims, preferred_element_type=F32)
    return multiply(first[0], second[0]) + (multiply(first[0], second[1]) + multiply(first[1], second[0]))


def swap(value):
    tiles = value.reshape(value.shape[0] // 8, 8, value.shape[1])
    return jnp.concatenate([tiles[:, 4:], tiles[:, :4]], 1).reshape(value.shape)


def real_rows(shape):
    return lax.broadcasted_iota(jnp.int32, shape, 0) % 8 < 4


def tables(energies):
    period = 2 * energies
    angle = np.outer(np.arange(period), np.arange(energies)) % period * (2.0 * math.pi / period)

    def ordered(real_real, real_imag, imag_real, imag_imag):
        grid = np.array([[real_real, real_imag], [imag_real, imag_imag]])
        rows, columns = real_real.shape
        grid = grid.reshape(2, 2, rows // 4, 4, columns // 4, 4).transpose(2, 0, 3, 4, 1, 5)
        return grid.reshape(2 * rows, 2 * columns)

    cos, sin = np.cos(angle), np.sin(angle)
    scale = 1.0 / (period * energies)
    result = []
    for table in (ordered(cos, sin, -sin, cos), scale * ordered(cos.T, -sin.T, sin.T, cos.T)):
        table = table.astype(np.float32)
        high = table.astype(BF16)
        result += [high, (table - high.astype(np.float32)).astype(BF16)]
    return result


def kernel(
    green_in, coulomb_in, offsets_in, retarded_in, fwd_hi_in, fwd_lo_in, inv_hi_in, inv_lo_in, out,
    green, retarded, fwd_hi, fwd_lo, inv_hi, inv_lo, offsets,
    pack, pairs, lhat, psend, precv, below, above, vboth, vhi, vlo, sel, yy, zsend, srecv, qsend, qhalo, xsend, sig,
    left_hi, left_lo, right_hi, right_lo,
    load_sem, local_sem, small_send, small_recv, send_sem, a_sem, p_sem, up_sem, down_sem, s_sem, q_sem, h_sem, x_sem, halo_sem, fwd_sem,
):
    wide, cell = lax.axis_index("wide"), lax.axis_index("cell")
    cells = lax.axis_size("cell")
    nx, nh, nc = WIDE_PARTS
    ny = 2 * nh
    group = nx * nc
    plane = ny * group
    order = green.shape[-1]
    core, yh, x = wide % nc, wide // nc % nh, wide // (nc * nh)
    yl, z = cell % 2, cell // 2
    y = 2 * yh + yl
    place = (y * nx + x) * nc + core
    up, down = (wide, (cell + 2) % cells), (wide, (cell + cells - 2) % cells)
    has_up, has_down = z < cells // 2 - 1, z > 0
    partner = (wide, cell + 1 - 2 * yl)

    def rows8(index):
        return pl.ds(pl.multiple_of(8 * index, 8), 8)

    def rise(g):
        k = ny - 1 - g
        return jnp.where(k % 2 == 1, (k + 1) // 2, (ny - k // 2) % ny)

    columns = [((x + h // nc) % nx, (core + h % nc) % nc) for h in range(group)]
    columns = [(x2 * nh * nc + c2, x2 * nc + c2) for x2, c2 in columns]

    def each_peer(act):
        def at(g, first):
            y2 = y + rise(g)
            y2 = jnp.where(y2 >= ny, y2 - ny, y2)
            yh2 = y2 // 2
            act(g, [(yh2 * nc + w, y2 * group + p) for w, p in columns[first:]], y2 - 2 * yh2)

        def step(g, carry):
            at(g, 0)
            return carry

        lax.fori_loop(0, ny - 1, step, 0)
        at(ny - 1, 1)

    def remote(src, dst, send, recv, device):
        return pltpu.make_async_remote_copy(
            src_ref=src, dst_ref=dst, send_sem=send, recv_sem=recv, device_id=device, device_id_type=MESH
        )

    def await_bytes(like, sem):
        pltpu.make_async_copy(like, like, sem).wait()

    def chunk(g):
        y0 = (y + ny - rise(g)) % ny
        return pl.ds(pl.multiple_of(y0 * (8 * group), 8 * group), 8 * group)

    def exchange(source, target, send, recv_of):
        def act(g, devices, yl2):
            for wide2, place2 in devices:
                remote(source(place2), target, send, recv_of(g), (wide2, 2 * z + yl2)).start()

        each_peer(act)

    others = pl.ds(0, 8 * plane - 8)

    loads = [
        pltpu.make_async_copy(src, dst, load_sem.at[i])
        for i, (src, dst) in enumerate((
            (green_in, green), (coulomb_in, vboth.at[yl]), (offsets_in, offsets), (fwd_hi_in, fwd_hi),
            (fwd_lo_in, fwd_lo), (inv_hi_in, inv_hi), (inv_lo_in, inv_lo), (retarded_in, retarded),
        ))
    ]
    for load in loads:
        load.start()

    barrier = pltpu.get_barrier_semaphore()

    def greet(g, devices, yl2):
        for wide2, place2 in devices:
            pl.semaphore_signal(barrier, inc=1, device_id=(wide2, 2 * z + yl2), device_id_type=MESH)

    each_peer(greet)
    for device, there in ((up, has_up), (down, has_down)):
        @pl.when(there)
        def _():
            pl.semaphore_signal(barrier, inc=1, device_id=device, device_id_type=MESH)

    even_sends, even_receives = jnp.logical_and(yl == 0, has_up), jnp.logical_and(yl == 0, has_down)
    loads[0].wait()

    def pack_half(i):
        for pair in range(2):
            for part in range(2):
                for e in range(LOCAL):
                    pack[i, pair, pl.ds(4 * part + e, plane, stride=8), :] = green[
                        pair, part, e, i * plane : (i + 1) * plane, :
                    ]

    pack_half(0)
    pl.semaphore_wait(barrier, plane - 1 + jnp.where(has_up, 1, 0) + jnp.where(has_down, 1, 0))

    own = []
    for i in range(2):
        if i == 1:
            pack_half(1)
        exchange(
            lambda place2: pack.at[i, :, rows8(place2), :], pairs.at[i, :, yl, rows8(wide), :],
            send_sem.at[0], lambda g: a_sem.at[i],
        )
        own.append(pltpu.make_async_copy(
            pack.at[i, :, rows8(place), :], pairs.at[i, :, yl, rows8(wide), :], local_sem.at[i]
        ))
        own[i].start()
    for load in loads[1:]:
        load.wait()
    for slot in range(2):
        sel[yl, slot] = jnp.where(jnp.full((8, order), offsets[0, slot], jnp.int32) != 0, 1.0, 0.0)
    coulomb_copy = remote(vboth.at[yl], vboth.at[yl], small_send.at[0], small_recv.at[0], partner)
    coulomb_copy.start()
    masks_copy = remote(sel.at[yl], sel.at[yl], small_send.at[1], small_recv.at[1], partner)
    masks_copy.start()

    @pl.when(jnp.logical_not(has_down))
    def _():
        below[...] = jnp.zeros_like(below)

    @pl.when(jnp.logical_not(has_up))
    def _():
        above[...] = jnp.zeros_like(above)
        qhalo[...] = jnp.zeros_like(qhalo)

    @pl.when(jnp.logical_and(yl == 0, jnp.logical_not(has_down)))
    def _():
        sig[0] = jnp.zeros(sig.shape[1:], F32)

    tile = min(128, fwd_hi.shape[0])
    for i in range(2):
        own[i].wait()
        await_bytes(pack.at[i, :, others, :], a_sem.at[i])

        def transform(r, carry):
            lesser, greater = pairs[i, 0, r], pairs[i, 1, r]
            conjugate = jnp.where(real_rows(greater.shape), greater, -greater)
            rhs = split(jnp.concatenate([lesser, conjugate], 1))
            for m in range(fwd_hi.shape[0] // tile):
                rows = slice(m * tile, (m + 1) * tile)
                both = dot3((fwd_hi[rows], fwd_lo[rows]), rhs)
                first, second = both[:, :order], both[:, order:]
                lhat[i, r, rows, :] = first
                same, cross = first * second, first * swap(second)
                psend[i, r, rows, :] = jnp.where(real_rows(same.shape), same + swap(same), cross - swap(cross))
            return carry

        lax.fori_loop(0, 2, transform, 0)
        exchange(
            lambda place2: psend.at[i, :, rows8(place2), :], precv.at[i, :, rows8(place), :],
            send_sem.at[1], lambda g: p_sem.at[i, g],
        )
        pltpu.make_async_copy(
            psend.at[i, :, rows8(place), :], precv.at[i, :, rows8(place), :], p_sem.at[i, ny - 1]
        ).start()

    coulomb_copy.wait()
    masks_copy.wait()
    for r in range(2):
        for slot in range(2):
            high, low = split(vboth[r, slot])
            vhi[r, :, slot * order : (slot + 1) * order] = high
            vlo[r, :, slot * order : (slot + 1) * order] = low

    def prepare(e, carry):
        for slot in range(2):
            at = 2 * e + slot
            (rh, rl), (ih, il) = split(retarded[0, e, slot]), split(retarded[1, e, slot])
            for left, right, real, imag in ((left_hi, right_hi, rh, ih), (left_lo, right_lo, rl, il)):
                left[at, :, :order] = real
                left[at, :, order:] = imag
                right[at, :order, :order] = real
                right[at, :order, order:] = -imag
                right[at, order:, :order] = imag
                right[at, order:, order:] = real
        return carry

    lax.fori_loop(0, LOCAL, prepare, 0)

    for i in range(2):
        def forward(g, carry):
            rows = chunk(g)
            await_bytes(precv.at[i, :, rows, :], p_sem.at[i, g])

            @pl.when(has_up)
            def _():
                remote(precv.at[i, 1, rows, :], below.at[i, rows, :], fwd_sem.at[0], up_sem.at[i, g], up).start()

            @pl.when(has_down)
            def _():
                remote(precv.at[i, 0, rows, :], above.at[i, rows, :], fwd_sem.at[1], down_sem.at[i, g], down).start()

            return carry

        lax.fori_loop(0, ny, forward, 0)

    full = 8 * plane
    part_rows = min(256, full)
    own = {}
    for r, halo, there, sems in ((1, above, has_up, down_sem), (0, below, has_down, up_sem)):
        for i in range(2):
            @pl.when(there)
            def _():
                def arrive(g, carry):
                    await_bytes(halo.at[i, chunk(g), :], sems.at[i, g])
                    return carry

                lax.fori_loop(0, ny, arrive, 0)

            def from_right(m, carry):
                rows = pl.ds(pl.multiple_of(m * part_rows, part_rows), part_rows)
                other, odd = halo[i, rows, :], precv[i, 1, rows, :]
                if r == 1:
                    first = jnp.where(sel[1, 0, 0:1, :] > 0.5, precv[i, 0, rows, :], odd)
                    second = jnp.where(sel[1, 1, 0:1, :] > 0.5, other, odd)
                else:
                    first, second = other, odd
                for slot, value in ((0, first), (1, second)):
                    block = slice(slot * order, (slot + 1) * order)
                    yy[r, slot, i, rows, :] = dot3(split(value), (vhi[r, :, block], vlo[r, :, block]), True)
                return carry

            lax.fori_loop(0, full // part_rows, from_right, 0)

        def from_left(t, carry):
            sides = []
            for part in range(2):
                sides.append(jnp.concatenate(
                    [yy[r, slot, i, pl.ds(4 * part + t, plane, stride=8), :] for slot in range(2) for i in range(2)], 0
                ))
            done = dot3((vhi[r], vlo[r]), split(jnp.concatenate(sides, 1)))
            for part in range(2):
                for i in range(2):
                    zsend[r, i, pl.ds(4 * part + t, plane, stride=8), :] = done[
                        i * plane : (i + 1) * plane, part * order : (part + 1) * order
                    ]
            return carry

        for t in range(LOCAL):
            from_left(t, 0)
        exchange(
            lambda place2: zsend.at[r, :, rows8(place2), :], srecv.at[r, :, rows8(place), :],
            send_sem.at[2], lambda g: s_sem.at[r],
        )
        own[r] = pltpu.make_async_copy(
            zsend.at[r, :, rows8(place), :], srecv.at[r, :, rows8(place), :], local_sem.at[2 + r]
        )
        own[r].start()

    def self_energy(r):
        own[r].wait()
        await_bytes(zsend.at[r, :, others, :], s_sem.at[r])
        sides = []
        for i in range(2):
            first, second = lhat[i, r], srecv[r, i]
            same, cross = first * second, first * swap(second)
            sides.append(jnp.where(real_rows(same.shape), same - swap(same), cross + swap(cross)))
        rhs = split(jnp.concatenate(sides, 1))
        tile = min(128, inv_hi.shape[0])
        for m in range(inv_hi.shape[0] // tile):
            rows = slice(m * tile, (m + 1) * tile)
            done = dot3((inv_hi[rows], inv_lo[rows]), rhs)
            for i in range(2):
                qsend[r, i, rows, :] = done[:, i * order : (i + 1) * order]

    def send_sigma(source, slot, parity, send, recv_of):
        def act(g, devices, yl2):
            @pl.when(yl2 == parity)
            def _():
                for wide2, place2 in devices:
                    remote(
                        source.at[:, rows8(wide2), :], sig.at[slot, :, rows8(place), :],
                        send, recv_of(g), (wide2, 2 * z + parity),
                    ).start()

        each_peer(act)

        @pl.when(yl == parity)
        def _():
            pltpu.make_async_copy(
                source.at[:, rows8(wide), :], sig.at[slot, :, rows8(place), :], recv_of(ny - 1)
            ).start()

    self_energy(1)
    send_sigma(qsend.at[1], 1, 0, send_sem.at[3], lambda g: q_sem.at[g])
    self_energy(0)

    @pl.when(has_down)
    def _():
        remote(qsend.at[0], qhalo, fwd_sem.at[3], halo_sem, down).start()

    xsend[0] = jnp.where(sel[1, 0, 0:1, :] > 0.5, qsend[0], qsend[1])
    send_sigma(xsend.at[0], 0, 1, send_sem.at[4], lambda g: x_sem.at[0])

    def spread(g, carry):
        rows = chunk(g)
        await_bytes(sig.at[1, :, rows, :], q_sem.at[g])

        @pl.when(has_up)
        def _():
            remote(sig.at[1, :, rows, :], sig.at[0, :, rows, :], fwd_sem.at[2], h_sem.at[g], up).start()

        return carry

    @pl.when(yl == 0)
    def _():
        lax.fori_loop(0, ny, spread, 0)

    @pl.when(has_up)
    def _():
        await_bytes(qhalo, halo_sem)

    xsend[1] = jnp.where(sel[1, 1, 0:1, :] > 0.5, qhalo[...], qsend[1])
    send_sigma(xsend.at[1], 1, 1, send_sem.at[5], lambda g: x_sem.at[1])

    def term(at, real, imag):
        left = dot3(
            (left_hi[at], left_lo[at]),
            split(jnp.concatenate([jnp.concatenate([real, imag], 1), jnp.concatenate([-imag, real], 1)], 0)),
        )
        return dot3(split(left), (right_hi[at], right_lo[at]), True)

    def dress(e, slot):
        real, imag = (
            jnp.concatenate([sig[slot, i, pl.ds(4 * part + e, plane, stride=8), :] for i in range(2)], 0)
            for part in range(2)
        )
        return term(2 * e + slot, real, imag)

    @pl.when(yl == 1)
    def _():
        await_bytes(sig.at[0], x_sem.at[0])

    for e in range(LOCAL):
        done = dress(e, 1 - yl)
        out[0, e] = done[:, :order]
        out[1, e] = done[:, order:]

    @pl.when(yl == 1)
    def _():
        await_bytes(sig.at[1], x_sem.at[1])

    def arrive_far(g, carry):
        await_bytes(sig.at[0, :, chunk(g), :], h_sem.at[g])
        return carry

    @pl.when(even_receives)
    def _():
        lax.fori_loop(0, ny, arrive_far, 0)

    for e in range(LOCAL):
        done = dress(e, yl)
        out[0, e] += done[:, :order]
        out[1, e] += done[:, order:]

    for phase, ref in enumerate((pack, psend, zsend)):
        await_bytes(ref.at[:, :, others, :], send_sem.at[phase])
    for parity in range(2):
        @pl.when(yl == parity)
        def _():
            for phase in (3, 4, 5):
                fewer = 8 if (phase == 3) == (parity == 0) else 0
                await_bytes(sig.at[0, :, pl.ds(0, 4 * plane - fewer), :], send_sem.at[phase])

    @pl.when(has_up)
    def _():
        await_bytes(below, fwd_sem.at[0])

    @pl.when(has_down)
    def _():
        await_bytes(above, fwd_sem.at[1])
        await_bytes(qhalo, fwd_sem.at[3])

    @pl.when(even_sends)
    def _():
        await_bytes(sig.at[0], fwd_sem.at[2])


def body(green_pair, coulomb, green_retarded, offsets):
    nx, nh, nc = WIDE_PARTS
    ny, plane = 2 * nh, 2 * nx * nh * nc
    order, local = green_pair.shape[-1], green_pair.shape[2]
    energies = local * nx * nh * nc
    full = 8 * plane
    consts = [jnp.asarray(value) for value in tables(energies)]
    hbm = pl.BlockSpec(memory_space=pltpu.HBM)
    arguments = (green_pair[:, :, :, 0], coulomb[0], offsets, green_retarded[:, :, 0], *consts)
    dma = pltpu.SemaphoreType.DMA
    dressed = pl.pallas_call(
        kernel,
        out_shape=jax.ShapeDtypeStruct((2, local, order, order), F32),
        in_specs=[hbm] * len(arguments),
        out_specs=pl.BlockSpec(memory_space=pltpu.VMEM),
        scratch_shapes=[
            pltpu.VMEM(arguments[0].shape, F32),
            pltpu.VMEM(arguments[3].shape, F32),
            *(pltpu.VMEM(value.shape, BF16) for value in consts),
            pltpu.SMEM((1, 2), jnp.int32),
            pltpu.VMEM((2, 2, full, order), F32),
            pltpu.VMEM((2, 2, 2, full // 2, order), F32),
            pltpu.VMEM((2, 2, full, order), F32),
            pltpu.VMEM((2, 2, full, order), F32),
            pltpu.VMEM((2, 2, full, order), F32),
            pltpu.VMEM((2, full, order), F32),
            pltpu.VMEM((2, full, order), F32),
            pltpu.VMEM((2, 2, order, order), F32),
            pltpu.VMEM((2, order, 2 * order), BF16),
            pltpu.VMEM((2, order, 2 * order), BF16),
            pltpu.VMEM((2, 2, 8, order), F32),
            pltpu.VMEM((2, 2, 2, full, order), F32),
            pltpu.VMEM((2, 2, full, order), F32),
            pltpu.VMEM((2, 2, full, order), F32),
            pltpu.VMEM((2, 2, full // 2, order), F32),
            pltpu.VMEM((2, full // 2, order), F32),
            pltpu.VMEM((2, 2, full // 2, order), F32),
            pltpu.VMEM((2, 2, full, order), F32),
            *[pltpu.VMEM((2 * local, order, 2 * order), BF16)] * 2,
            *[pltpu.VMEM((2 * local, 2 * order, 2 * order), BF16)] * 2,
            dma((8,)), dma((4,)), dma((2,)), dma((2,)), dma((6,)), dma((2,)), dma((2, ny)), dma((2, ny)), dma((2, ny)),
            dma((2,)), dma((ny,)), dma((ny,)), dma((2,)), dma, dma((4,)),
        ],
        compiler_params=pltpu.CompilerParams(
            collective_id=0, has_side_effects=True, vmem_limit_bytes=60 * 1024 * 1024
        ),
    )(*arguments)
    return dressed[:, :, None]


def solution(mesh):
    placed = (
        P(None, None, "wide", "cell", None, None),
        P("cell", None, None, None),
        P(None, "wide", "cell", None, None, None),
        P("cell", None),
    )
    return jax.shard_map(
        body,
        mesh=mesh,
        in_specs=placed,
        out_specs=P(None, "wide", "cell", None, None),
        check_vma=False,
    )
```
